32 devices in a mesh: tm: 8 (over z, x), chan: 4 (over y, core).
Axes of the slice: x: 2, y: 2, z: 4, core: 2. Of those that a mesh axis runs over, the one named last changes fastest.
Arguments:
- inputs: bfloat16 [16, 256, 512], P('tm'), may hold values from -6 to 6
- decay: float32 [16, 512], P('tm', 'chan'), may hold values from 0 to 1, as said below
- kernel_b: bfloat16 [9, 512, 256], P(None, 'chan'), may hold values from -0.125 to 0.125
- kernel_c: bfloat16 [9, 256, 512], P(None, 'chan'), may hold values from -0.09375 to 0.09375
- cotangent: bfloat16 [16, 256, 512], P('tm', 'chan'), may hold values from -0.0625 to 0.0625
Outputs:
- grad_b: float32 [9, 512, 256], P(None, 'chan')
- grad_c: float32 [9, 256, 512], P(None, 'chan')
- decay_grad: float32 [16, 512], P('tm', 'chan')
The draws below stay inside these ranges and needn't reach their ends.
Inputs may be any that keep to these rules, and one draw needn't show every extreme that they name: decay lies strictly between 0 and 1.
All inputs are finite; a program needn't handle non-finite values.
Results may differ from the reference program's by a relative error of at most 0.003.
Values may be sent and summed in bfloat16 or wider, within the bound.
A program may use at most 128 MiB of HBM per device.

```python
import jax
import jax.numpy as jnp
from jax import lax

U = 256
STATE_CHANNELS = 512
W = 64
H = 8
TOTAL_FRAMES = 16


def draw_decay(key, part):
    random_keys = jax.random.split(key, 6)
    slow_share = 5
    slow = jax.random.randint(random_keys[0], (STATE_CHANNELS,), 0, 10) < slow_share
    rate_slow = jax.random.uniform(random_keys[1], (STATE_CHANNELS,), jnp.float32, 0.3, 1.5) / TOTAL_FRAMES
    rate_fast = jax.random.uniform(random_keys[2], (STATE_CHANNELS,), jnp.float32, 0.15, 0.5)
    rates = jnp.where(slow, rate_slow, rate_fast)
    jitter = jnp.exp(jax.random.uniform(random_keys[3], (TOTAL_FRAMES, STATE_CHANNELS), jnp.float32, -0.35, 0.35))
    frame_groups = jax.random.randint(random_keys[4], (3,), 0, TOTAL_FRAMES)
    marked_rows = jnp.any(jnp.arange(TOTAL_FRAMES)[:, None] == frame_groups[None, :], axis=1)
    depth = jax.random.uniform(random_keys[5], (TOTAL_FRAMES, 1), jnp.float32, 0.5, 0.8)
    decay_factor = jnp.where(marked_rows[:, None], depth, 1.0)
    return (jnp.exp(-rates[None, :] * jitter) * decay_factor).astype(jnp.float32)


def shard_levels(rng, dims, shards, least, top_value):
    gain, own = 1.0, jax.random.fold_in(rng, 6)
    for position, shards_of in shards:
        draws = jnp.exp(jax.random.uniform(jax.random.fold_in(own, position), (shards_of,), jnp.float32, least / len(shards), top_value / len(shards)))
        gain = gain * jnp.repeat(draws, dims[position] // shards_of).reshape([-1 if axis == position else 1 for axis in range(len(dims))])
    return gain


def centred(key, extent, scale, reach, shards=(), kind=jnp.bfloat16):
    result = jax.random.normal(key, extent, jnp.float32) * scale
    if len(shards) > 0:
        result = shard_levels(key, extent, shards, -0.22, 0.18) * result
    return jnp.clip(result, min=-reach, max=reach).astype(kind)


def setup_inputs(seed: int = 0) -> dict:
    splits = jax.random.split(jax.random.key(seed), 6)
    inputs = centred(splits[0], (TOTAL_FRAMES, U, H * W), 1.0, 6.0, ((0, 8),))
    decay = draw_decay(jax.random.fold_in(splits[5], 71), 0)
    kernel_b = centred(splits[2], (9, STATE_CHANNELS, U), (9 * U) ** -0.5, 0.125, ((1, 4),))
    kernel_c = centred(splits[3], (9, U, STATE_CHANNELS), (9 * STATE_CHANNELS) ** -0.5, 0.09375, ((1, 4),))
    cotangent = centred(splits[4], (TOTAL_FRAMES, U, H * W), ((TOTAL_FRAMES * H * W) ** -0.5), 0.0625, ((0, 8), (1, 4)))
    return {"inputs": inputs, "decay": decay, "kernel_b": kernel_b, "kernel_c": kernel_c, "cotangent": cotangent}


offsets = ((-1, -1), (-1, 0), (-1, 1), (0, -1), (0, 0), (0, 1), (1, -1), (1, 0), (1, 1))


def shift_cells(source, row_shift, col_shift, grid_width):
    cell_count = source.shape[-1]
    margin = grid_width + 1
    padded = jnp.pad(source, [(0, 0)] * (source.ndim - 1) + [(margin, margin)])
    first_cell = margin + row_shift * grid_width + col_shift
    shifted = lax.slice_in_dim(padded, first_cell, first_cell + cell_count, axis=source.ndim - 1)
    column = jnp.arange(cell_count) % grid_width
    inside = (column + col_shift >= 0) & (column + col_shift < grid_width)
    return jnp.where(inside, shifted, jnp.zeros((), source.dtype))


def stencil_stack(source, grid_width, decay_factor):
    parts = [shift_cells(source, decay_factor * pair[0], decay_factor * pair[1], grid_width) for pair in offsets]
    return jnp.stack(parts, axis=source.ndim - 2)


def reference(inputs, decay, kernel_b, kernel_c, cotangent):
    weight_b = kernel_b.astype(jnp.float32)
    weight_c = kernel_c.astype(jnp.float32)
    cell_count = inputs.shape[-1]

    def advance(current, frame_pair):
        input_frame, frame_rate = frame_pair
        input_stack = stencil_stack(input_frame, W, 1).astype(jnp.float32)
        drive = jnp.einsum('kpc,kcs->ps', weight_b, input_stack)
        current = frame_rate[:, None] * current + drive
        return current, current

    final_state, states = lax.scan(advance, jnp.zeros((STATE_CHANNELS, cell_count), jnp.float32), (inputs, decay))
    previous = jnp.concatenate([jnp.zeros((1, STATE_CHANNELS, cell_count), jnp.float32), states[:-1]], axis=0)

    def retreat(carry_all, frame_pair):
        carried, grad_b, grad_c = carry_all
        input_frame, frame_rate, frame_cot, frame_state, frame_prev = frame_pair
        cot_stack = stencil_stack(frame_cot, W, -1).astype(jnp.float32)
        injected = jnp.einsum('kup,kus->ps', weight_c, cot_stack)
        adjoint = injected + carried
        adjoint_bf = lax.optimization_barrier(adjoint.astype(jnp.bfloat16)).astype(jnp.float32)
        input_stack = stencil_stack(input_frame, W, 1).astype(jnp.float32)
        grad_b = grad_b + jnp.einsum('ps,kcs->kpc', adjoint_bf, input_stack)
        state_bf = lax.optimization_barrier(frame_state.astype(jnp.bfloat16)).astype(jnp.float32)
        state_stack = stencil_stack(state_bf, W, 1)
        grad_c = grad_c + jnp.einsum('us,kps->kup', frame_cot.astype(jnp.float32), state_stack)
        decay_row = jnp.sum(adjoint * frame_prev, axis=1)
        return (frame_rate[:, None] * adjoint, grad_b, grad_c), decay_row

    start = (jnp.zeros((STATE_CHANNELS, cell_count), jnp.float32), jnp.zeros((9, STATE_CHANNELS, U), jnp.float32), jnp.zeros((9, U, STATE_CHANNELS), jnp.float32))
    ending, decay_grad = lax.scan(retreat, start, (inputs, decay, cotangent, states, previous), reverse=True)
    return ending[1], ending[2], decay_grad
```

```python
import jax
import jax.numpy as jnp
from jax import lax
from jax.experimental import pallas as pl
from jax.experimental.pallas import tpu as pltpu
from jax.sharding import PartitionSpec as P

W = 64
ROWS = 16
MESH = pl.DeviceIdType.MESH
F32 = jnp.float32
BF16 = jnp.bfloat16

offsets = ((-1, -1), (-1, 0), (-1, 1), (0, -1), (0, 0), (0, 1), (1, -1), (1, 0), (1, 1))


def nt(a, b):
    return lax.dot_general(a, b, (((1,), (1,)), ((), ())), preferred_element_type=F32)


def build_stack(source, stack, sign, block=32):
    frames, channels, cells = source.shape
    blocks = channels // block
    cell = lax.broadcasted_iota(jnp.int32, (1, cells), 1)
    column = cell % W
    masks = []
    for dr, dc in offsets:
        dr, dc = sign * dr, sign * dc
        ok = (column + dc >= 0) & (column + dc < W)
        there = cell + dr * W
        masks.append(ok & (there >= 0) & (there < cells))

    def step(index, carry):
        frame = index // blocks
        row = pl.multiple_of((index % blocks) * block, block)
        lane = pl.multiple_of(frame * cells, cells)
        z = source[frame, pl.ds(row, block), :].astype(F32)
        for k, (dr, dc) in enumerate(offsets):
            by = (-sign * (dr * W + dc)) % cells
            moved = z if by == 0 else pltpu.roll(z, by, 1)
            moved = jnp.where(masks[k], moved, 0.0).astype(BF16)
            stack[pl.ds(pl.multiple_of(k * channels + row, block), block), pl.ds(lane, cells)] = moved
        return carry

    lax.fori_loop(0, frames * blocks, step, 0)


def kernel(n, nc, x_ref, decay_ref, kb_ref, kc_ref, cot_ref,
           gb_out, gc_out, dg_out,
           xs, cs, kbt, kct, kcg, cotg, dr, inj, ent, arr, ebuf, mbuf, erecv, mrecv, eres, mres,
           gcb, gbb, gcrecv, gbrecv, gcred, gbred, gcx,
           cot_s, cot_r, kc_s, kc_r, e_s, e_r, m_s, m_r, ent_s, ent_r, arr_s, arr_r,
           gcs_s, gcs_r, gbs_s, gbs_r, gcx_s, gcx_r, gca_s, gca_r, gba_s, gba_r):
    me = lax.axis_index("tm")
    ch = lax.axis_index("chan")
    frames, channels, cells = x_ref.shape
    taps = kb_ref.shape[0]
    p = kb_ref.shape[1]
    ul = kc_ref.shape[1]
    owners = p // ROWS
    stride = n // owners
    mine = me // stride
    per = gcb.shape[1] // owners
    pending = []

    def on_owner(fn):
        if stride == 1:
            fn()
        else:
            pl.when(lax.rem(me, stride) == 0)(fn)

    def off_owner(fn):
        if stride > 1:
            pl.when(lax.rem(me, stride) != 0)(fn)

    barrier = pltpu.get_barrier_semaphore()
    for d in range(1, n):
        pl.semaphore_signal(barrier, inc=1, device_id={"tm": lax.rem(me + d, n)}, device_id_type=MESH)
    for d in range(1, nc):
        pl.semaphore_signal(barrier, inc=1, device_id={"chan": lax.rem(ch + d, nc)}, device_id_type=MESH)
    pl.semaphore_wait(barrier, n + nc - 2)

    def remote(src, dst, s, r, to):
        return pltpu.make_async_remote_copy(src_ref=src, dst_ref=dst, send_sem=s, recv_sem=r,
                                            device_id=to, device_id_type=MESH)

    def part(ref, c):
        return ref.at[pl.ds(pl.multiple_of(c * ROWS, ROWS), ROWS), :]

    def scatter(piece, recv, s, r):
        for d in range(1, owners):
            c = lax.rem(mine + d, owners)
            to = c * stride
            rel = lax.rem(me - to + n, n) if stride > 1 else n - d
            copy = remote(piece(c), recv.at[rel], s.at[d], r.at[rel], {"tm": to})
            copy.start()
            pending.append((copy, None))

        def near():
            rel = lax.rem(me, stride)
            copy = remote(piece(mine), recv.at[rel], s.at[0], r.at[rel], {"tm": mine * stride})
            copy.start()
            copy.wait_send()

        off_owner(near)

    def arrived(piece, recv, s, r):
        for rel in range(1, n):
            remote(piece(0), recv.at[rel], s.at[0], r.at[rel], {"tm": me}).wait_recv()

    def spread(src, dst, s, r):
        copies = []
        for d in range(1, n):
            copies.append(remote(src, dst(mine), s.at[d], r.at[mine], {"tm": lax.rem(me + d, n)}))
        for copy in copies:
            copy.start()
        return copies

    def spread_wait(src, dst, s, r):
        for d in range(1, owners):
            c = lax.rem(mine + d, owners)
            remote(src, dst(c), s.at[0], r.at[c], {"tm": me}).wait_recv()
        off_owner(lambda: remote(src, dst(mine), s.at[0], r.at[mine], {"tm": me}).wait_recv())

    urow = pl.multiple_of(ch * ul, ul)
    gathers = []
    for d in range(1, nc):
        to = lax.rem(ch + d, nc)
        copy = remote(cot_ref, cotg.at[:, pl.ds(urow, ul), :], cot_s.at[d], cot_r.at[d], {"chan": to})
        copy.start()
        gathers.append(copy)
        cols = pl.ds(pl.multiple_of(to * p, p), p)
        copy = remote(kc_ref.at[:, :, cols], kcg.at[:, pl.ds(urow, ul), :], kc_s.at[d], kc_r.at[d], {"chan": to})
        copy.start()
        gathers.append(copy)
    cotg[:, pl.ds(urow, ul), :] = cot_ref[...]
    kcg[:, pl.ds(urow, ul), :] = kc_ref[:, :, pl.ds(pl.multiple_of(ch * p, p), p)]

    rate = decay_ref[...]
    a0 = jnp.broadcast_to(rate[0:1], (128, p)).T
    a1 = jnp.broadcast_to(rate[1:2], (128, p)).T
    wide = lambda a: jnp.concatenate([a] * (cells // 128), axis=1)

    build_stack(x_ref, xs, 1)
    for k in range(taps):
        kbt[:, k * channels:(k + 1) * channels] = kb_ref[k]
    dr[...] = jnp.dot(kbt[...], xs[...], preferred_element_type=F32)
    ebuf[:, :cells] = wide(a1) * dr[:, :cells] + dr[:, cells:]
    ebuf[:, cells:] = a0 * a1
    scatter(lambda c: part(ebuf, c), erecv, e_s, e_r)

    for copy in gathers:
        copy.wait_recv()
    build_stack(cotg, cs, -1)
    for k in range(taps):
        kct[:, k * channels:(k + 1) * channels] = kcg[k].T

    def scan_forward():
        arrived(lambda c: part(ebuf, c), erecv, e_s, e_r)
        erecv[0] = ebuf[pl.ds(pl.multiple_of(mine * ROWS, ROWS), ROWS), :]
        carried = jnp.zeros((ROWS, cells), F32)
        for j in range(n):
            eres[j] = carried
            if j < n - 1:
                slot = lax.rem(j - me + n, n)
                carried = wide(erecv[slot, :, cells:]) * carried + erecv[slot, :, :cells]

    def scan_backward():
        arrived(lambda c: part(mbuf, c), mrecv, m_s, m_r)
        mrecv[0] = mbuf[pl.ds(pl.multiple_of(mine * ROWS, ROWS), ROWS), :]
        carried = jnp.zeros((ROWS, cells), F32)
        for j in range(n - 1, -1, -1):
            mres[j] = carried
            if j > 0:
                slot = lax.rem(j - me + n, n)
                carried = wide(erecv[slot, :, cells:]) * carried + mrecv[slot]

    def hand_back(res, dst, s, r):
        row = pl.multiple_of(mine * ROWS, ROWS)
        dst[pl.ds(row, ROWS), :] = res[me]
        for d in range(1, n):
            to = lax.rem(me + d, n)
            remote(res.at[to], part(dst, mine), s.at[d], r.at[mine], {"tm": to}).start()

    def handed(res, dst, s, r):
        spread_wait(res.at[0], lambda c: part(dst, c), s, r)

    def drain(src, s):
        for d in range(1, n):
            remote(src, src, s.at[d], s.at[d], {"tm": me}).wait_send()

    def forward():
        scan_forward()
        hand_back(eres, ent, ent_s, ent_r)

    on_owner(forward)

    inj[...] = jnp.dot(kct[...], cs[...], preferred_element_type=F32)
    mbuf[...] = wide(a0) * (inj[:, :cells] + wide(a1) * inj[:, cells:])
    scatter(lambda c: part(mbuf, c), mrecv, m_s, m_r)

    handed(eres, ent, ent_s, ent_r)
    s0 = wide(a0) * ent[...] + dr[:, :cells]
    s1 = wide(a1) * s0 + dr[:, cells:]
    dr[:, :cells] = s0
    states = jnp.concatenate([s0.astype(BF16), s1.astype(BF16)], axis=1)
    units = channels // ROWS // nc
    gcb[:, taps * units:] = jnp.zeros((nc, gcb.shape[1] - taps * units, ROWS, p), BF16)
    for k in range(taps):
        grad = nt(cs[k * channels:(k + 1) * channels, :], states).astype(BF16)
        gcb[:, k * units:(k + 1) * units] = grad.reshape(nc, units, ROWS, p)
    gc_piece = lambda c: gcb.at[:, pl.ds(c * per, per)]
    scatter(gc_piece, gcrecv, gcs_s, gcs_r)

    def backward():
        scan_backward()
        hand_back(mres, arr, arr_s, arr_r)

    on_owner(backward)

    handed(mres, arr, arr_s, arr_r)
    adj1 = inj[:, cells:] + arr[...]
    adj0 = inj[:, :cells] + wide(a1) * adj1
    inj[:, :cells] = adj0
    inj[:, cells:] = adj1
    adjoint = jnp.concatenate([adj0.astype(BF16), adj1.astype(BF16)], axis=1)
    for k in range(taps):
        gbb[k] = nt(adjoint, xs[k * channels:(k + 1) * channels, :]).astype(BF16)
    gb_piece = lambda c: gbb.at[:, pl.ds(pl.multiple_of(c * ROWS, ROWS), ROWS), :]
    scatter(gb_piece, gbrecv, gbs_s, gbs_r)

    gc_slot = lambda c: gc_out.at[:, pl.ds(c * per, per)]
    gb_slot = lambda c: gb_out.at[:, pl.ds(pl.multiple_of(c * ROWS, ROWS), ROWS), :]

    def reduce_gc():
        arrived(gc_piece, gcrecv, gcs_s, gcs_r)
        total = gcb[:, pl.ds(mine * per, per)].astype(F32)
        for rel in range(1, n):
            total = total + gcrecv[rel].astype(F32)
        gcred[...] = total.astype(BF16)
        gcx[ch] = gcred[ch]
        for d in range(1, nc):
            to = lax.rem(ch + d, nc)
            remote(gcred.at[to], gcx.at[ch], gcx_s.at[d], gcx_r.at[d], {"chan": to}).start()

    on_owner(reduce_gc)

    def fold(product):
        lanes = product[:, :128]
        for i in range(1, cells // 128):
            lanes = lanes + product[:, i * 128:(i + 1) * 128]
        return jnp.sum(lanes.T, axis=0, keepdims=True)

    dg_out[0:1, :] = fold(inj[:, :cells] * ent[...])
    dg_out[1:2, :] = fold(inj[:, cells:] * dr[:, :cells])

    def share_gc():
        for d in range(1, nc):
            remote(gcred.at[0], gcx.at[lax.rem(ch - d + nc, nc)], gcx_s.at[d], gcx_r.at[d], {"chan": ch}).wait()
        gc_out[:, pl.ds(mine * per, per)] = gcx[...]
        spread(gcx, gc_slot, gca_s, gca_r)

    on_owner(share_gc)

    def reduce_gb():
        arrived(gb_piece, gbrecv, gbs_s, gbs_r)
        row = pl.ds(pl.multiple_of(mine * ROWS, ROWS), ROWS)
        total = gbb[:, row, :].astype(F32)
        for rel in range(1, n):
            total = total + gbrecv[rel].astype(F32)
        gbred[...] = total.astype(BF16)
        gb_out[:, row, :] = gbred[...]
        spread(gbred, gb_slot, gba_s, gba_r)

    on_owner(reduce_gb)

    spread_wait(gcx, gc_slot, gca_s, gca_r)
    spread_wait(gbred, gb_slot, gba_s, gba_r)
    for copy in gathers:
        copy.wait_send()
    for copy, _ in pending:
        copy.wait_send()

    def owner_drain():
        drain(eres.at[0], ent_s)
        drain(mres.at[0], arr_s)
        drain(gcx, gca_s)
        drain(gbred, gba_s)

    on_owner(owner_drain)


def body(n, nc, inputs, decay, kernel_b, kernel_c, cotangent):
    frames, channels, cells = inputs.shape
    taps, p, _ = kernel_b.shape
    owners = p // ROWS
    units = taps * channels // ROWS // nc
    per = -(-units // owners)
    padded = per * owners
    span = frames * cells
    vm = pltpu.VMEM
    dma = lambda count: pltpu.SemaphoreType.DMA((count,))
    scratch = [
        vm((taps * channels, span), BF16), vm((taps * channels, span), BF16),
        vm((p, taps * channels), BF16), vm((p, taps * channels), BF16),
        vm((taps, channels, p), BF16), vm((frames, channels, cells), BF16),
        vm((p, span), F32), vm((p, span), F32),
        vm((p, cells), F32), vm((p, cells), F32),
        vm((p, cells + 128), F32), vm((p, cells), F32),
        vm((n, ROWS, cells + 128), F32), vm((n, ROWS, cells), F32),
        vm((n, ROWS, cells), F32), vm((n, ROWS, cells), F32),
        vm((nc, padded, ROWS, p), BF16), vm((taps, p, channels), BF16),
        vm((n, nc, per, ROWS, p), BF16), vm((n, taps, ROWS, channels), BF16),
        vm((nc, per, ROWS, p), BF16), vm((taps, ROWS, channels), BF16),
        vm((nc, per, ROWS, p), BF16),
        dma(nc), dma(nc), dma(nc), dma(nc),
        dma(owners), dma(n), dma(owners), dma(n),
        dma(n), dma(owners), dma(n), dma(owners),
        dma(owners), dma(n), dma(owners), dma(n),
        dma(nc), dma(nc),
        dma(n), dma(owners), dma(n), dma(owners),
    ]
    flops = 4 * 2 * p * taps * channels * span
    gb, gc, dg = pl.pallas_call(
        lambda *refs: kernel(n, nc, *refs),
        out_shape=(
            jax.ShapeDtypeStruct((taps, p, channels), BF16),
            jax.ShapeDtypeStruct((nc, padded, ROWS, p), BF16),
            jax.ShapeDtypeStruct(decay.shape, F32),
        ),
        in_specs=[pl.BlockSpec(memory_space=vm)] * 5,
        out_specs=(pl.BlockSpec(memory_space=vm),) * 3,
        scratch_shapes=scratch,
        compiler_params=pltpu.CompilerParams(
            collective_id=0, has_side_effects=True, vmem_limit_bytes=56 * 1024 * 1024
        ),
        cost_estimate=pl.CostEstimate(flops=flops, bytes_accessed=8 * 1024 * 1024, transcendentals=0),
    )(inputs, decay, kernel_b, kernel_c, cotangent)
    grad_c = gc[:, :units].reshape(nc, taps, channels // nc, p).transpose(1, 2, 0, 3)
    grad_c = grad_c.reshape(taps, channels // nc, nc * p).astype(F32)
    return gb.astype(F32), grad_c, dg


def solution(mesh):
    n, nc = mesh.shape["tm"], mesh.shape["chan"]
    in_specs = (
        P("tm", None, None),
        P("tm", "chan"),
        P(None, "chan", None),
        P(None, "chan", None),
        P("tm", "chan", None),
    )
    out_specs = (P(None, "chan", None), P(None, "chan", None), P("tm", "chan"))
    return jax.shard_map(lambda *args: body(n, nc, *args), mesh=mesh, in_specs=in_specs,
                         out_specs=out_specs, check_vma=False)
```

```python
import jax
import jax.numpy as jnp
from jax import lax
from jax.experimental import pallas as pl
from jax.experimental.pallas import tpu as pltpu
from jax.sharding import PartitionSpec as P

W = 64
ROWS = 16
MESH = pl.DeviceIdType.MESH
F32 = jnp.float32
BF16 = jnp.bfloat16

offsets = ((-1, -1), (-1, 0), (-1, 1), (0, -1), (0, 0), (0, 1), (1, -1), (1, 0), (1, 1))


def nt(a, b):
    return lax.dot_general(a, b, (((1,), (1,)), ((), ())), preferred_element_type=F32)


def build_stack(source, stack, sign, block=32):
    frames, channels, cells = source.shape
    blocks = channels // block
    cell = lax.broadcasted_iota(jnp.int32, (1, cells), 1)
    column = cell % W
    masks = []
    for dr, dc in offsets:
        dr, dc = sign * dr, sign * dc
        ok = (column + dc >= 0) & (column + dc < W)
        there = cell + dr * W
        masks.append(ok & (there >= 0) & (there < cells))

    def step(index, carry):
        frame = index // blocks
        row = pl.multiple_of((index % blocks) * block, block)
        lane = pl.multiple_of(frame * cells, cells)
        z = source[frame, pl.ds(row, block), :].astype(F32)
        for k, (dr, dc) in enumerate(offsets):
            by = (-sign * (dr * W + dc)) % cells
            moved = z if by == 0 else pltpu.roll(z, by, 1)
            moved = jnp.where(masks[k], moved, 0.0).astype(BF16)
            stack[pl.ds(pl.multiple_of(k * channels + row, block), block), pl.ds(lane, cells)] = moved
        return carry

    lax.fori_loop(0, frames * blocks, step, 0)


def kernel(n, nc, x_ref, decay_ref, kb_ref, kc_ref, cot_ref,
           gb_out, gc_out, dg_out,
           xs, cs, kbt, kct, kcg, cotg, dr, inj, ent, arr, ebuf, mbuf, erecv, mrecv, eres, mres,
           gcb, gbb, gcrecv, gbrecv, gcred, gbred, gcx,
           cot_s, cot_r, kc_s, kc_r, e_s, e_r, m_s, m_r, ent_s, ent_r, arr_s, arr_r,
           gcs_s, gcs_r, gbs_s, gbs_r, gcx_s, gcx_r, gca_s, gca_r, gba_s, gba_r):
    me = lax.axis_index("tm")
    ch = lax.axis_index("chan")
    frames, channels, cells = x_ref.shape
    taps = kb_ref.shape[0]
    p = kb_ref.shape[1]
    ul = kc_ref.shape[1]
    owners = p // ROWS
    stride = n // owners
    mine = me // stride
    per = gcb.shape[1] // owners
    pending = []

    def on_owner(fn):
        if stride == 1:
            fn()
        else:
            pl.when(lax.rem(me, stride) == 0)(fn)

    def off_owner(fn):
        if stride > 1:
            pl.when(lax.rem(me, stride) != 0)(fn)

    barrier = pltpu.get_barrier_semaphore()
    for d in range(1, n):
        pl.semaphore_signal(barrier, inc=1, device_id={"tm": lax.rem(me + d, n)}, device_id_type=MESH)
    for d in range(1, nc):
        pl.semaphore_signal(barrier, inc=1, device_id={"chan": lax.rem(ch + d, nc)}, device_id_type=MESH)
    pl.semaphore_wait(barrier, n + nc - 2)

    def remote(src, dst, s, r, to):
        return pltpu.make_async_remote_copy(src_ref=src, dst_ref=dst, send_sem=s, recv_sem=r,
                                            device_id=to, device_id_type=MESH)

    def part(ref, c):
        return ref.at[pl.ds(pl.multiple_of(c * ROWS, ROWS), ROWS), :]

    def scatter(piece, recv, s, r):
        for d in range(1, owners):
            c = lax.rem(mine + d, owners)
            to = c * stride
            rel = lax.rem(me - to + n, n) if stride > 1 else n - d
            copy = remote(piece(c), recv.at[rel], s.at[d], r.at[rel], {"tm": to})
            copy.start()
            pending.append((copy, None))

        def near():
            rel = lax.rem(me, stride)
            copy = remote(piece(mine), recv.at[rel], s.at[0], r.at[rel], {"tm": mine * stride})
            copy.start()
            copy.wait_send()

        off_owner(near)

    def arrived(piece, recv, s, r):
        for rel in range(1, n):
            remote(piece(0), recv.at[rel], s.at[0], r.at[rel], {"tm": me}).wait_recv()

    staged = stride == 1 and n % 2 == 0 and n > 2
    beside = me + 1 - 2 * lax.rem(me, 2)

    def spread(src, dst, s, r):
        if staged:
            remote(src, dst(mine), s.at[n // 2], r.at[mine], {"tm": beside}).start()
            for d in range(1, n // 2):
                remote(src, dst(mine), s.at[d], r.at[mine], {"tm": lax.rem(me + 2 * d, n)}).start()
        else:
            for d in range(1, n):
                remote(src, dst(mine), s.at[d], r.at[mine], {"tm": lax.rem(me + d, n)}).start()

    def pass_on(src, dst, s, r):
        if staged:
            for d in range(1, n // 2):
                c = lax.rem(me - 2 * d + n, n)
                remote(src, dst(c), s.at[0], r.at[c], {"tm": me}).wait_recv()
                remote(dst(c), dst(c), s.at[n // 2 + d], r.at[c], {"tm": beside}).start()

    def spread_rest(src, dst, s, r):
        if staged:
            for d in range(n // 2):
                c = lax.rem(beside - 2 * d + n, n)
                remote(src, dst(c), s.at[0], r.at[c], {"tm": me}).wait_recv()
        else:
            spread_wait(src, dst, s, r)

    def spread_wait(src, dst, s, r):
        for d in range(1, owners):
            c = lax.rem(mine + d, owners)
            remote(src, dst(c), s.at[0], r.at[c], {"tm": me}).wait_recv()
        off_owner(lambda: remote(src, dst(mine), s.at[0], r.at[mine], {"tm": me}).wait_recv())

    urow = pl.multiple_of(ch * ul, ul)
    gathers = []
    for d in range(1, nc):
        to = lax.rem(ch + d, nc)
        copy = remote(cot_ref, cotg.at[:, pl.ds(urow, ul), :], cot_s.at[d], cot_r.at[d], {"chan": to})
        copy.start()
        gathers.append(copy)
        cols = pl.ds(pl.multiple_of(to * p, p), p)
        copy = remote(kc_ref.at[:, :, cols], kcg.at[:, pl.ds(urow, ul), :], kc_s.at[d], kc_r.at[d], {"chan": to})
        copy.start()
        gathers.append(copy)
    cotg[:, pl.ds(urow, ul), :] = cot_ref[...]
    kcg[:, pl.ds(urow, ul), :] = kc_ref[:, :, pl.ds(pl.multiple_of(ch * p, p), p)]

    rate = decay_ref[...]
    a0 = jnp.broadcast_to(rate[0:1], (128, p)).T
    a1 = jnp.broadcast_to(rate[1:2], (128, p)).T
    wide = lambda a: jnp.concatenate([a] * (cells // 128), axis=1)

    build_stack(x_ref, xs, 1)
    for k in range(taps):
        kbt[:, k * channels:(k + 1) * channels] = kb_ref[k]
    dr[...] = jnp.dot(kbt[...], xs[...], preferred_element_type=F32)
    ebuf[:, :cells] = wide(a1) * dr[:, :cells] + dr[:, cells:]
    ebuf[:, cells:] = a0 * a1
    scatter(lambda c: part(ebuf, c), erecv, e_s, e_r)

    for copy in gathers:
        copy.wait_recv()
    build_stack(cotg, cs, -1)
    for k in range(taps):
        kct[:, k * channels:(k + 1) * channels] = kcg[k].T

    def scan_forward():
        arrived(lambda c: part(ebuf, c), erecv, e_s, e_r)
        erecv[0] = ebuf[pl.ds(pl.multiple_of(mine * ROWS, ROWS), ROWS), :]
        carried = jnp.zeros((ROWS, cells), F32)
        for j in range(n):
            eres[j] = carried
            if j < n - 1:
                slot = lax.rem(j - me + n, n)
                carried = wide(erecv[slot, :, cells:]) * carried + erecv[slot, :, :cells]

    def scan_backward():
        arrived(lambda c: part(mbuf, c), mrecv, m_s, m_r)
        mrecv[0] = mbuf[pl.ds(pl.multiple_of(mine * ROWS, ROWS), ROWS), :]
        carried = jnp.zeros((ROWS, cells), F32)
        for j in range(n - 1, -1, -1):
            mres[j] = carried
            if j > 0:
                slot = lax.rem(j - me + n, n)
                carried = wide(erecv[slot, :, cells:]) * carried + mrecv[slot]

    def hand_back(res, dst, s, r):
        row = pl.multiple_of(mine * ROWS, ROWS)
        dst[pl.ds(row, ROWS), :] = res[me]
        for d in range(1, n):
            to = lax.rem(me + d, n)
            remote(res.at[to], part(dst, mine), s.at[d], r.at[mine], {"tm": to}).start()

    def handed(res, dst, s, r):
        spread_wait(res.at[0], lambda c: part(dst, c), s, r)

    def drain(src, s):
        for d in range(1, n):
            remote(src, src, s.at[d], s.at[d], {"tm": me}).wait_send()

    def forward():
        scan_forward()
        hand_back(eres, ent, ent_s, ent_r)

    on_owner(forward)

    inj[...] = jnp.dot(kct[...], cs[...], preferred_element_type=F32)
    mbuf[...] = wide(a0) * (inj[:, :cells] + wide(a1) * inj[:, cells:])
    scatter(lambda c: part(mbuf, c), mrecv, m_s, m_r)

    handed(eres, ent, ent_s, ent_r)
    s0 = wide(a0) * ent[...] + dr[:, :cells]
    s1 = wide(a1) * s0 + dr[:, cells:]
    dr[:, :cells] = s0
    states = jnp.concatenate([s0.astype(BF16), s1.astype(BF16)], axis=1)
    units = channels // ROWS // nc
    gcb[:, taps * units:] = jnp.zeros((nc, gcb.shape[1] - taps * units, ROWS, p), BF16)
    for k in range(taps):
        grad = nt(cs[k * channels:(k + 1) * channels, :], states).astype(BF16)
        gcb[:, k * units:(k + 1) * units] = grad.reshape(nc, units, ROWS, p)
    gc_piece = lambda c: gcb.at[:, pl.ds(c * per, per)]
    scatter(gc_piece, gcrecv, gcs_s, gcs_r)

    def backward():
        scan_backward()
        hand_back(mres, arr, arr_s, arr_r)

    on_owner(backward)

    handed(mres, arr, arr_s, arr_r)
    adj1 = inj[:, cells:] + arr[...]
    adj0 = inj[:, :cells] + wide(a1) * adj1
    inj[:, :cells] = adj0
    inj[:, cells:] = adj1
    adjoint = jnp.concatenate([adj0.astype(BF16), adj1.astype(BF16)], axis=1)
    for k in range(taps):
        gbb[k] = nt(adjoint, xs[k * channels:(k + 1) * channels, :]).astype(BF16)
    gb_piece = lambda c: gbb.at[:, pl.ds(pl.multiple_of(c * ROWS, ROWS), ROWS), :]
    scatter(gb_piece, gbrecv, gbs_s, gbs_r)

    gc_slot = lambda c: gc_out.at[:, pl.ds(c * per, per)]
    gb_slot = lambda c: gb_out.at[:, pl.ds(pl.multiple_of(c * ROWS, ROWS), ROWS), :]

    def reduce_gc():
        arrived(gc_piece, gcrecv, gcs_s, gcs_r)
        total = gcb[:, pl.ds(mine * per, per)].astype(F32)
        for rel in range(1, n):
            total = total + gcrecv[rel].astype(F32)
        gcred[...] = total.astype(BF16)
        gcx[ch] = gcred[ch]
        for d in range(1, nc):
            to = lax.rem(ch + d, nc)
            remote(gcred.at[to], gcx.at[ch], gcx_s.at[d], gcx_r.at[d], {"chan": to}).start()

    on_owner(reduce_gc)

    def fold(product):
        lanes = product[:, :128]
        for i in range(1, cells // 128):
            lanes = lanes + product[:, i * 128:(i + 1) * 128]
        return jnp.sum(lanes.T, axis=0, keepdims=True)

    dg_out[0:1, :] = fold(inj[:, :cells] * ent[...])
    dg_out[1:2, :] = fold(inj[:, cells:] * dr[:, :cells])

    def share_gc():
        for d in range(1, nc):
            remote(gcred.at[0], gcx.at[lax.rem(ch - d + nc, nc)], gcx_s.at[d], gcx_r.at[d], {"chan": ch}).wait()
        gc_out[:, pl.ds(mine * per, per)] = gcx[...]
        spread(gcx, gc_slot, gca_s, gca_r)

    on_owner(share_gc)

    def reduce_gb():
        arrived(gb_piece, gbrecv, gbs_s, gbs_r)
        row = pl.ds(pl.multiple_of(mine * ROWS, ROWS), ROWS)
        total = gbb[:, row, :].astype(F32)
        for rel in range(1, n):
            total = total + gbrecv[rel].astype(F32)
        gbred[...] = total.astype(BF16)
        gb_out[:, row, :] = gbred[...]
        spread(gbred, gb_slot, gba_s, gba_r)

    on_owner(reduce_gb)

    pass_on(gcx, gc_slot, gca_s, gca_r)
    pass_on(gbred, gb_slot, gba_s, gba_r)
    spread_rest(gcx, gc_slot, gca_s, gca_r)
    spread_rest(gbred, gb_slot, gba_s, gba_r)
    for copy in gathers:
        copy.wait_send()
    for copy, _ in pending:
        copy.wait_send()

    def owner_drain():
        drain(eres.at[0], ent_s)
        drain(mres.at[0], arr_s)
        drain(gcx, gca_s)
        drain(gbred, gba_s)

    on_owner(owner_drain)


def body(n, nc, inputs, decay, kernel_b, kernel_c, cotangent):
    frames, channels, cells = inputs.shape
    taps, p, _ = kernel_b.shape
    owners = p // ROWS
    units = taps * channels // ROWS // nc
    per = -(-units // owners)
    padded = per * owners
    span = frames * cells
    vm = pltpu.VMEM
    dma = lambda count: pltpu.SemaphoreType.DMA((count,))
    scratch = [
        vm((taps * channels, span), BF16), vm((taps * channels, span), BF16),
        vm((p, taps * channels), BF16), vm((p, taps * channels), BF16),
        vm((taps, channels, p), BF16), vm((frames, channels, cells), BF16),
        vm((p, span), F32), vm((p, span), F32),
        vm((p, cells), F32), vm((p, cells), F32),
        vm((p, cells + 128), F32), vm((p, cells), F32),
        vm((n, ROWS, cells + 128), F32), vm((n, ROWS, cells), F32),
        vm((n, ROWS, cells), F32), vm((n, ROWS, cells), F32),
        vm((nc, padded, ROWS, p), BF16), vm((taps, p, channels), BF16),
        vm((n, nc, per, ROWS, p), BF16), vm((n, taps, ROWS, channels), BF16),
        vm((nc, per, ROWS, p), BF16), vm((taps, ROWS, channels), BF16),
        vm((nc, per, ROWS, p), BF16),
        dma(nc), dma(nc), dma(nc), dma(nc),
        dma(owners), dma(n), dma(owners), dma(n),
        dma(n), dma(owners), dma(n), dma(owners),
        dma(owners), dma(n), dma(owners), dma(n),
        dma(nc), dma(nc),
        dma(n), dma(owners), dma(n), dma(owners),
    ]
    flops = 4 * 2 * p * taps * channels * span
    gb, gc, dg = pl.pallas_call(
        lambda *refs: kernel(n, nc, *refs),
        out_shape=(
            jax.ShapeDtypeStruct((taps, p, channels), BF16),
            jax.ShapeDtypeStruct((nc, padded, ROWS, p), BF16),
            jax.ShapeDtypeStruct(decay.shape, F32),
        ),
        in_specs=[pl.BlockSpec(memory_space=vm)] * 5,
        out_specs=(pl.BlockSpec(memory_space=vm),) * 3,
        scratch_shapes=scratch,
        compiler_params=pltpu.CompilerParams(
            collective_id=0, has_side_effects=True, vmem_limit_bytes=56 * 1024 * 1024
        ),
        cost_estimate=pl.CostEstimate(flops=flops, bytes_accessed=8 * 1024 * 1024, transcendentals=0),
    )(inputs, decay, kernel_b, kernel_c, cotangent)
    grad_c = gc[:, :units].reshape(nc, taps, channels // nc, p).transpose(1, 2, 0, 3)
    grad_c = grad_c.reshape(taps, channels // nc, nc * p).astype(F32)
    return gb.astype(F32), grad_c, dg


def solution(mesh):
    n, nc = mesh.shape["tm"], mesh.shape["chan"]
    in_specs = (
        P("tm", None, None),
        P("tm", "chan"),
        P(None, "chan", None),
        P(None, "chan", None),
        P("tm", "chan", None),
    )
    out_specs = (P(None, "chan", None), P(None, "chan", None), P("tm", "chan"))
    return jax.shard_map(lambda *args: body(n, nc, *args), mesh=mesh, in_specs=in_specs,
                         out_specs=out_specs, check_vma=False)
```
